32 devices in a mesh: expert: 8 (over y, x, core), dp: 4 (over z).
Axes of the slice: x: 2, y: 2, z: 4, core: 2. Of those that a mesh axis runs over, the one named last changes fastest.
Arguments:
- tokens: bfloat16 [4096, 2048], P(('expert', 'dp')), may hold values from -6 to 6
- cotangent: bfloat16 [4096, 2048], P(('expert', 'dp')), may hold values from -6 to 6
- routes: int32 [4096, 4], P(('expert', 'dp')), may hold values from 0 to 7, all different within a row; in each aligned block of 128 rows (0 to 127, 128 to 255, ...) at most 96 rows name the same one
- gate_values: bfloat16 [4096, 4], P(('expert', 'dp')), may hold values from 0.099609375 to 1
- w_gate: bfloat16 [8, 2048, 512], P('expert', 'dp'), may hold values from -0.125 to 0.125
- w_up: bfloat16 [8, 2048, 512], P('expert', 'dp'), may hold values from -0.125 to 0.125
- w_down: bfloat16 [8, 512, 2048], P('expert', None, 'dp'), may hold values from -0.25 to 0.25
Outputs:
- token_grad: bfloat16 [4096, 2048], P(('expert', 'dp'))
- gate_weight_grad: bfloat16 [8, 2048, 512], P('expert', 'dp')
- up_weight_grad: bfloat16 [8, 2048, 512], P('expert', 'dp')
- down_weight_grad: bfloat16 [8, 512, 2048], P('expert', None, 'dp')
The draws below stay inside these ranges and needn't reach their ends.
Inputs may be any that keep to these rules, and one draw needn't show every extreme that they name: `routes`: each row names 4 different experts. Among the rows of one device no expert is named more than 96 times, and some device names some expert exactly 96 times.
All inputs are finite; a program needn't handle non-finite values.
Results may differ from the reference program's by a relative error of at most 0.017.
Values may be sent and summed in bfloat16 or wider, within the bound.
A program may use at most 128 MiB of HBM per device.

```python
import math
import jax
import jax.numpy as jnp
import numpy as np
from jax import lax

D = 2048
FF = 512
TOP = 4
TOK_DEV = 128
EXPERTS = 8
CAP = 96
TOKENS = 4096
N_EXPERT = 8
N_DP = 4


def block_scale(key, dims, pieces, low, top_value):
    level, own = 1.0, jax.random.fold_in(key, 6)
    for dim, blocks in pieces:
        steps = jnp.exp(jax.random.uniform(jax.random.fold_in(own, dim), (blocks,), jnp.float32, low / len(pieces), top_value / len(pieces)))
        level = level * jnp.repeat(steps, dims[dim] // blocks).reshape([-1 if axis == dim else 1 for axis in range(len(dims))])
    return level


def assign_block(stream_key, own, number, rows, number_of, top, most, skew):
    sequence = jax.random.permutation(stream_key, number_of)
    crowded, ordinary = load_shares(number_of, rows * top, most, skew, True), load_shares(number_of, rows * top, most, skew, False)
    places = jnp.arange(number_of)

    def named(lengths, turn):
        used = int((lengths > 0).sum())
        fixed = max(1, used // 4)
        passed = fixed + (places - fixed + turn * (used - fixed)) % max(1, number_of - fixed)
        return jnp.zeros((number_of,), jnp.int32).at[sequence[jnp.where(places < fixed, places, passed)]].set(jnp.asarray(lengths, jnp.int32))

    lengths = jnp.where(number % 4 == 0, named(crowded, number // 4), named(ordinary, number - number // 4 - 1))
    mixed = jax.random.permutation(jax.random.fold_in(own, 3), number_of)
    source_of, taker = mixed[0:number_of // 2 * 2:2], mixed[1:number_of // 2 * 2:2]
    room = jnp.minimum(lengths[source_of] - 1, most - lengths[taker]) // 2
    room = jnp.where((source_of == sequence[0]) | (taker == sequence[0]) | (lengths[taker] == 0), 0, jnp.maximum(room, 0))
    passed = jax.random.randint(jax.random.fold_in(own, 4), (number_of // 2,), 0, 1 << 20) % (room + 1)
    lengths = lengths.at[source_of].add(-passed).at[taker].add(passed)
    items = jnp.searchsorted(jnp.cumsum(lengths), jnp.arange(rows * top), side="right").astype(jnp.int32)
    table = items.reshape(top, rows).T
    table = table[jax.random.permutation(jax.random.fold_in(own, 1), rows)]
    turn = jax.random.randint(jax.random.fold_in(own, 2), (rows, 1), 0, top)
    return jnp.take_along_axis(table, (jnp.arange(top)[None, :] + turn) % top, axis=1)


def load_shares(amount, total, most, skew, full):
    loads = [(1 << 20) // math.isqrt(rank ** skew) + 1 for rank in range(1, amount + 1)]
    largest = most if full else min(most, max(-(-total // amount), total * loads[0] // sum(loads)))
    least = 1 if total - largest >= amount - 1 else 0
    holding, rest = [largest] + [least] * (amount - 1), total - largest - least * (amount - 1)
    while rest > 0:
        free = [i for i in range(1, amount) if holding[i] < largest] or [i for i in range(1, amount) if holding[i] < most]
        pool, left = sum([loads[i] for i in free]), rest
        for i in free:
            addition = min(most - holding[i], max(1, left * loads[i] // pool), rest)
            holding[i] = holding[i] + addition
            rest = rest - addition
    return np.array(holding)


def gaussian(key, extent, spread, bound, shards=(), kind=jnp.bfloat16):
    values = jax.random.normal(key, extent, jnp.float32) * spread
    if len(shards) > 0:
        values = block_scale(key, extent, shards, -0.22, 0.18) * values
    return jnp.clip(values, min=-bound, max=bound).astype(kind)


def setup_inputs(seed: int = 0) -> dict:
    splits = jax.random.split(jax.random.key(seed), 8)
    tokens = gaussian(splits[0], (TOKENS, D), 1.0, 6.0, ((0, 32),))
    cotangent = gaussian(splits[1], (TOKENS, D), 1.0, 6.0, ((0, 32),))
    routes_keys = jax.random.split(jax.random.fold_in(splits[2], 1), TOKENS // TOK_DEV)
    routes_turns = jax.random.permutation(jax.random.fold_in(splits[2], 3), TOKENS // TOK_DEV)
    routes = jax.vmap(lambda own, number: assign_block(jax.random.fold_in(splits[2], 2), own, number, TOK_DEV, EXPERTS, TOP, CAP, 2))(routes_keys, routes_turns).reshape((TOKENS, TOP))
    gate_values = jnp.clip(jnp.exp(math.log(1.0) - 2.306499 * jax.random.uniform(splits[3], (TOKENS, TOP), jnp.float32) ** block_scale(splits[3], (TOKENS, TOP), ((0, 32),), -0.2, 0.2)), 0.099609375, 1.0).astype(jnp.bfloat16)
    w_gate = gaussian(splits[4], (EXPERTS, D, FF), D ** -0.5, 0.125, ((0, 8), (1, 4)))
    w_up = gaussian(splits[5], (EXPERTS, D, FF), D ** -0.5, 0.125, ((0, 8), (1, 4)))
    w_down = gaussian(splits[6], (EXPERTS, FF, D), FF ** -0.5, 0.25, ((0, 8), (2, 4)))
    return {"tokens": tokens, "cotangent": cotangent, "routes": routes, "gate_values": gate_values, "w_gate": w_gate, "w_up": w_up, "w_down": w_down}


def expert_pass(x_rows, dy_rows, gate_rows, weight_gate, weight_up, weight_down):
    gate_pre = jnp.dot(x_rows, weight_gate, preferred_element_type=jnp.float32)
    up_pre = jnp.dot(x_rows, weight_up, preferred_element_type=jnp.float32)
    sigmoid_gate = 1.0 / (1.0 + jnp.exp(-gate_pre))
    activated = gate_pre * sigmoid_gate
    hidden = (activated * up_pre).astype(jnp.bfloat16)
    scaled = (gate_rows[:, None].astype(jnp.float32) * dy_rows.astype(jnp.float32)).astype(jnp.bfloat16)
    hidden_grad = lax.dot_general(scaled, weight_down, (((1,), (1,)), ((), ())), preferred_element_type=jnp.float32)
    gate_grad = (hidden_grad * up_pre * sigmoid_gate * (1.0 + gate_pre * (1.0 - sigmoid_gate))).astype(jnp.bfloat16)
    up_grad = (hidden_grad * activated).astype(jnp.bfloat16)
    row_grad = lax.dot_general(gate_grad, weight_gate, (((1,), (1,)), ((), ())), preferred_element_type=jnp.float32)
    row_grad = row_grad + lax.dot_general(up_grad, weight_up, (((1,), (1,)), ((), ())), preferred_element_type=jnp.float32)
    return hidden, scaled, gate_grad, up_grad, row_grad.astype(jnp.bfloat16)


def group_sum(left, right):
    left_groups = left.reshape(N_DP, -1, left.shape[1]).astype(jnp.float32)
    right_groups = right.reshape(N_DP, -1, right.shape[1]).astype(jnp.float32)
    partial_sums = jnp.einsum("prd,prf->pdf", left_groups, right_groups)
    rounded = lax.optimization_barrier(partial_sums.astype(jnp.bfloat16))
    return jnp.sum(rounded.astype(jnp.float32), axis=0).astype(jnp.bfloat16)


def reference(tokens, cotangent, routes, gate_values, w_gate, w_up, w_down):
    blocks = N_EXPERT * N_DP
    per_expert = N_DP * N_EXPERT * CAP
    expert_ids = routes.reshape(blocks, TOK_DEV * TOP).astype(jnp.int32)
    onehot = (expert_ids[:, :, None] == jnp.arange(EXPERTS, dtype=jnp.int32)[None, None, :]).astype(jnp.int32)
    before = jnp.cumsum(onehot, axis=1) - onehot
    slot = jnp.sum(before * onehot, axis=2).astype(jnp.int32)
    block_ids = jnp.arange(blocks, dtype=jnp.int32)[:, None]
    source_dev = block_ids // N_DP
    group_ids = block_ids % N_DP
    position = (group_ids * N_EXPERT + source_dev) * CAP + slot
    flat_dest = (expert_ids * per_expert + position).reshape(-1).astype(jnp.int32)
    assigns = TOKENS * TOP
    row_index = jnp.full((EXPERTS * per_expert,), assigns, jnp.int32).at[flat_dest].set(jnp.arange(assigns, dtype=jnp.int32))
    tokens_pad = jnp.concatenate([tokens, jnp.zeros((1, D), tokens.dtype)], axis=0)
    cot_pad = jnp.concatenate([cotangent, jnp.zeros((1, D), cotangent.dtype)], axis=0)
    gate_pad = jnp.concatenate([gate_values.reshape(-1), jnp.zeros((1,), gate_values.dtype)], axis=0)

    def one_expert(inputs):
        indices, weight_gate, weight_up, weight_down = inputs
        token_ids = (indices // TOP).astype(jnp.int32)
        x_rows = tokens_pad[token_ids]
        dy_rows = cot_pad[token_ids]
        gate_rows = gate_pad[indices]
        hidden, scaled, gate_grad, up_grad, row_grad = expert_pass(x_rows, dy_rows, gate_rows, weight_gate, weight_up, weight_down)
        return group_sum(x_rows, gate_grad), group_sum(x_rows, up_grad), group_sum(hidden, scaled), row_grad

    grad_gate, grad_up, grad_down, row_grads = lax.map(one_expert, (row_index.reshape(EXPERTS, per_expert), w_gate, w_up, w_down))
    all_rows = row_grads.reshape(EXPERTS * per_expert, D)
    dest_table = flat_dest.reshape(TOKENS, TOP)
    summed = jnp.zeros((TOKENS, D), jnp.float32)
    for which in range(TOP):
        summed = summed + all_rows[dest_table[:, which]].astype(jnp.float32)
    return summed.astype(jnp.bfloat16), grad_gate, grad_up, grad_down
```

```python
import jax
import jax.numpy as jnp
from jax import lax
from jax.experimental import pallas as pl
from jax.experimental.pallas import tpu as pltpu
from jax.sharding import PartitionSpec as P

MESH = pl.DeviceIdType.MESH
BF16 = jnp.bfloat16
F32 = jnp.float32
CHUNKS = 4
GATE_LANES = 128


def contract(left, right, dims):
    return lax.dot_general(left, right, ((dims[:1], dims[1:]), ((), ())), preferred_element_type=F32)


def moe_kernel(
    tok_in, cot_in, gate_in, wg_in, wu_in, wd_in,
    tok_out, gg_out, gu_out, gd_out,
    rows, scaled, w1, w2, p1, p2, b1, b2, total, gu, hid,
    pair_send, pair_recv, chip_sum, diag_recv, near_recv,
    load_sem, ag_send, ag_recv, rs_send, rs_recv, tok_send, tok_recv, ret_send, ret_recv,
):
    e, z = lax.axis_index("expert"), lax.axis_index("dp")
    n_dev, tok_dev, width = scaled.shape
    chunks, n_z, depth, fc2 = w1.shape
    fc = fc2 // 2
    last = n_z - 1
    core, x, y = e % 2, (e // 2) % 2, e // 4
    partner = e + 1 - 2 * core
    near_x = e + 2 - 4 * x
    near_y = e + 4 - 8 * y
    diag = near_x + 4 - 8 * y
    half = tok_dev // 2

    loads = [
        pltpu.make_async_copy(tok_in, rows.at[e, :, pl.ds(0, width)], load_sem.at[0]),
        pltpu.make_async_copy(cot_in, rows.at[e, :, pl.ds(width, width)], load_sem.at[1]),
        pltpu.make_async_copy(gate_in, rows.at[e, :, pl.ds(2 * width, GATE_LANES)], load_sem.at[2]),
    ]
    for f in range(chunks):
        cols = pl.ds(f * fc, fc)
        k = 3 + 3 * f
        loads += [
            pltpu.make_async_copy(wg_in.at[:, cols], w1.at[f, z, :, pl.ds(0, fc)], load_sem.at[k]),
            pltpu.make_async_copy(wu_in.at[:, cols], w1.at[f, z, :, pl.ds(fc, fc)], load_sem.at[k + 1]),
            pltpu.make_async_copy(wd_in.at[cols, :], w2.at[f, z], load_sem.at[k + 2]),
        ]
    for load in loads:
        load.start()

    barrier = pltpu.get_barrier_semaphore()
    for near in (partner, near_x, near_y):
        pl.semaphore_signal(barrier, inc=1, device_id=(near, z), device_id_type=MESH)

    @pl.when(z > 0)
    def _():
        pl.semaphore_signal(barrier, inc=1, device_id=(e, z - 1), device_id_type=MESH)

    @pl.when(z < last)
    def _():
        pl.semaphore_signal(barrier, inc=1, device_id=(e, z + 1), device_id_type=MESH)

    for load in loads:
        load.wait()
    pl.semaphore_wait(barrier, 3 + jnp.minimum(z, 1) + jnp.minimum(last - z, 1))

    def remote(src, dst, send, recv, target):
        return pltpu.make_async_remote_copy(
            src_ref=src, dst_ref=dst, send_sem=send, recv_sem=recv, device_id=target, device_id_type=MESH
        )

    def ag_pair(f, way, s, block):
        target = (e, z + 1) if way == 0 else (e, z - 1)
        return [
            remote(w.at[f, block], w.at[f, block], ag_send.at[f, way, s, i], ag_recv.at[f, way, s, i], target)
            for i, w in enumerate((w1, w2))
        ]

    def ag_sends(f, way, s):
        ok = (z >= s) & (z < last) if way == 0 else (z + s <= last) & (z > 0)
        block = jnp.clip(z - s if way == 0 else z + s, 0, last)
        return ok, ag_pair(f, way, s, block)

    def ag_start(f, s):
        for way in range(2):
            ok, copies = ag_sends(f, way, s)

            @pl.when(ok)
            def _():
                for copy in copies:
                    copy.start()

    def ag_wait(f, s):
        for way in range(2):
            block = z - 1 - s if way == 0 else z + 1 + s
            ok = block >= 0 if way == 0 else block <= last
            copies = ag_pair(f, way, s, jnp.clip(block, 0, last))

            @pl.when(ok)
            def _():
                for copy in copies:
                    copy.wait_recv()

    def rs_pair(f, way, s, block):
        target = (e, z + 1) if way == 0 else (e, z - 1)
        return [
            remote(p.at[f, block], b.at[f, way, s], rs_send.at[f, way, s, i], rs_recv.at[f, way, s, i], target)
            for i, (p, b) in enumerate(((p1, b1), (p2, b2)))
        ]

    def rs_place(way, s):
        place = z if way == 0 else last - z
        block = jnp.clip(last + z - s if way == 0 else s + z - last, 0, last)
        return place, block

    def add_in(dst, src):
        step = 64

        @pl.loop(0, dst.shape[0] // step)
        def _(i):
            at = pl.ds(pl.multiple_of(i * step, step), step)
            dst[at, :] = (dst[at, :].astype(F32) + src[at, :].astype(F32)).astype(BF16)

    def rs_take(f, way, s, block):
        for copy in rs_pair(f, way, s, block):
            copy.wait_recv()
        add_in(p1.at[f, block], b1.at[f, way, s])
        add_in(p2.at[f, block], b2.at[f, way, s])

    def rs_slot(f, s, also):
        for way in range(2):
            place, block = rs_place(way, s)
            if s > 0:

                @pl.when(also & (s >= place) & (place > 0))
                def _():
                    rs_take(f, way, s - 1, block)

            @pl.when(also & (s >= place))
            def _():
                for copy in rs_pair(f, way, s, block):
                    copy.start()

    def rs_end(f):
        for way in range(2):
            place, _block = rs_place(way, 0)

            @pl.when(place > 0)
            def _():
                rs_take(f, way, last - 1, z)

    lo, hi = pl.ds(0, half), pl.ds(half, half)

    def rows_copy(block, k, target, part=None):
        ref = rows.at[block] if part is None else rows.at[block, part]
        return remote(ref, ref, tok_send.at[k], tok_recv.at[k], (target, z))

    flip = 1 - 2 * core
    own_sends = [rows_copy(e, 0, near_x), rows_copy(e, 1, near_y), rows_copy(e, 4, partner)]
    first_recv = [rows_copy(near_x, 0, near_x), rows_copy(near_y, 1, near_y)]
    second_sends = [
        rows_copy(near_x, 2, near_y, lo), rows_copy(near_y, 3, near_x, hi),
        rows_copy(near_x, 5, partner), rows_copy(near_y, 6, partner),
    ]
    second_recv = [rows_copy(diag, 2, near_y, lo), rows_copy(diag, 3, near_x, hi)]
    third_sends = [rows_copy(diag, 7, partner)]
    third_recv = [
        rows_copy(partner, 4, partner), rows_copy(near_x + flip, 5, partner),
        rows_copy(near_y + flip, 6, partner), rows_copy(diag + flip, 7, partner),
    ]

    def scale_block(d, carry):
        lanes = lax.broadcasted_iota(jnp.int32, (tok_dev, GATE_LANES), 1)
        gates = rows[d, :, 2 * width : 2 * width + GATE_LANES].astype(F32)
        gate = jnp.sum(jnp.where(lanes == e, gates, 0.0), axis=1, keepdims=True)
        scaled[d] = (gate * rows[d, :, width : 2 * width].astype(F32)).astype(BF16)
        return carry

    def forward_tile(f, i):
        at = pl.ds(2 * i, 2)
        tile = 2 * tok_dev
        x_rows = rows[at, :, 0:width].reshape(tile, width)
        pre = jnp.dot(x_rows, w1[f].reshape(width, fc2), preferred_element_type=F32)
        hidden_grad = jnp.zeros((tile, fc), F32)
        for b in range(n_z):
            dy = scaled[at, :, b * depth : (b + 1) * depth].reshape(tile, depth)
            hidden_grad += contract(dy, w2[f, b], (1, 1))
        gate_pre, up_pre = pre[:, :fc], pre[:, fc:]
        sig = 1.0 / (1.0 + jnp.exp(-gate_pre))
        act = gate_pre * sig
        hid[at] = (act * up_pre).astype(BF16).reshape(2, tok_dev, fc)
        gate_grad = (hidden_grad * up_pre * sig * (1.0 + gate_pre * (1.0 - sig))).astype(BF16)
        gu[at, :, 0:fc] = gate_grad.reshape(2, tok_dev, fc)
        gu[at, :, fc:fc2] = (hidden_grad * act).astype(BF16).reshape(2, tok_dev, fc)

    def weight_grads(f):
        all_rows = n_dev * tok_dev
        for b in range(n_z):
            cut = slice(b * depth, (b + 1) * depth)
            x_cut = rows[:, :, cut].reshape(all_rows, depth)
            p1[f, b] = contract(x_cut, gu[...].reshape(all_rows, fc2), (0, 0)).astype(BF16)
            dy_cut = scaled[:, :, cut].reshape(all_rows, depth)
            p2[f, b] = contract(hid[...].reshape(all_rows, fc), dy_cut, (0, 0)).astype(BF16)

    def row_tile(f, i):
        at = pl.ds(2 * i, 2)
        left = gu[at].reshape(2 * tok_dev, fc2)
        for b in range(n_z):
            part = contract(left, w1[f, b], (1, 1)).reshape(2, tok_dev, depth)
            cut = slice(b * depth, (b + 1) * depth)

            @pl.when(f == 0)
            def _():
                total[at, :, cut] = part

            @pl.when(f > 0)
            def _():
                total[at, :, cut] = total[at, :, cut] + part

    ag_start(0, 0)
    for copy in own_sends:
        copy.start()

    @pl.loop(0, chunks)
    def _(f):
        before = jnp.maximum(f - 1, 0)
        for s in range(n_z - 1):
            ag_wait(f, s)
            if s < n_z - 2:
                ag_start(f, s + 1)
            if s == n_z - 3:

                @pl.when(f + 1 < chunks)
                def _():
                    ag_start(jnp.minimum(f + 1, chunks - 1), 0)

            if s > 0:
                rs_slot(before, s, f > 0)

            @pl.when(f == 0)
            def _():
                if s == 0:
                    for i in range(2):
                        first_recv[i].wait_recv()
                        second_sends[i].start()
                        second_sends[i + 2].start()
                elif s == 1:
                    for copy in second_recv:
                        copy.wait_recv()
                    third_sends[0].start()
                elif s == n_z - 2:
                    for copy in third_recv:
                        copy.wait_recv()
                    lax.fori_loop(0, n_dev, scale_block, 0)

        @pl.when(f > 0)
        def _():
            rs_end(before)

        @pl.loop(0, n_dev // 2)
        def _(i):
            forward_tile(f, i)

        weight_grads(f)
        rs_slot(f, 0, f >= 0)

        @pl.loop(0, n_dev // 2)
        def _(i):
            row_tile(f, i)

    final = chunks - 1
    places = [(e, partner), (near_x, near_x + flip), (near_y, near_y + flip), (diag, diag + flip)]

    def pair_copy(k):
        return remote(pair_send.at[k], pair_recv.at[k], ret_send.at[k], ret_recv.at[k], (partner, z))

    for k in (3, 1, 2, 0):
        pair_send[k] = total[places[k][1]].astype(BF16)
        pair_copy(k).start()
    rs_slot(final, 1, final >= 0)
    for k in (3, 1, 2, 0):
        pair_copy(k).wait_recv()
        chip_sum[k] = (total[places[k][0]] + pair_recv[k].astype(F32)).astype(BF16).reshape(2, half, width)
        if k == 3:
            diag_copies = [
                remote(chip_sum.at[3, 0], diag_recv.at[0], ret_send.at[4], ret_recv.at[4], (near_x, z)),
                remote(chip_sum.at[3, 1], diag_recv.at[1], ret_send.at[5], ret_recv.at[5], (near_y, z)),
            ]
            for copy in diag_copies:
                copy.start()
    near_copies = [
        remote(chip_sum.at[1, 0], near_recv.at[0, 0], ret_send.at[6], ret_recv.at[6], (near_x, z)),
        remote(chip_sum.at[2, 1], near_recv.at[1, 1], ret_send.at[7], ret_recv.at[7], (near_y, z)),
        remote(chip_sum.at[2, 0], near_recv.at[1, 0], ret_send.at[8], ret_recv.at[8], (near_y, z)),
        remote(chip_sum.at[1, 1], near_recv.at[0, 1], ret_send.at[9], ret_recv.at[9], (near_x, z)),
    ]
    near_copies[0].start()
    near_copies[1].start()
    diag_copies[0].wait_recv()
    add_in(chip_sum.at[2, 0], diag_recv.at[0])
    near_copies[2].start()
    diag_copies[1].wait_recv()
    add_in(chip_sum.at[1, 1], diag_recv.at[1])
    near_copies[3].start()
    for s in range(2, n_z - 1):
        rs_slot(final, s, final >= 0)
    for copy in near_copies:
        copy.wait_recv()
    for h in range(2):
        tok_out[h * half : (h + 1) * half, :] = (
            chip_sum[0, h].astype(F32) + near_recv[0, h].astype(F32) + near_recv[1, h].astype(F32)
        ).astype(BF16)
    rs_end(final)
    for f in range(chunks):
        cols = slice(f * fc, (f + 1) * fc)
        gg_out[:, cols] = p1[f, z, :, 0:fc]
        gu_out[:, cols] = p1[f, z, :, fc:fc2]
        gd_out[cols, :] = p2[f, z]

    @pl.loop(0, chunks)
    def _(f):
        for way in range(2):
            for s in range(n_z - 1):
                ok, copies = ag_sends(f, way, s)

                @pl.when(ok)
                def _():
                    for copy in copies:
                        copy.wait_send()

                place, block = rs_place(way, s)

                @pl.when(s >= place)
                def _():
                    for copy in rs_pair(f, way, s, block):
                        copy.wait_send()

    for copy in own_sends + second_sends + third_sends + diag_copies + near_copies:
        copy.wait_send()
    for k in range(4):
        pair_copy(k).wait_send()


def one_kernel(tokens, cotangent, routes, gate_values, w_gate, w_up, w_down):
    experts, n_z = lax.axis_size("expert"), lax.axis_size("dp")
    tok_dev, width = tokens.shape
    depth, ff = w_gate.shape[1:]
    fc = ff // CHUNKS
    lanes = jnp.arange(GATE_LANES, dtype=jnp.int32)
    named = routes[:, :, None] == lanes[None, None, :]
    gates = jnp.sum(jnp.where(named, gate_values[:, :, None].astype(F32), 0.0), axis=1).astype(BF16)
    dma = pltpu.SemaphoreType.DMA
    hops = n_z - 1
    any_spec, vmem_spec = pl.BlockSpec(memory_space=pl.ANY), pl.BlockSpec(memory_space=pltpu.VMEM)
    token_grad, gate_grad, up_grad, down_grad = pl.pallas_call(
        moe_kernel,
        out_shape=(
            jax.ShapeDtypeStruct((tok_dev, width), BF16),
            jax.ShapeDtypeStruct((depth, ff), BF16),
            jax.ShapeDtypeStruct((depth, ff), BF16),
            jax.ShapeDtypeStruct((ff, depth), BF16),
        ),
        in_specs=[any_spec] * 6,
        out_specs=(vmem_spec,) * 4,
        scratch_shapes=[
            pltpu.VMEM((experts, tok_dev, 2 * width + GATE_LANES), BF16),
            pltpu.VMEM((experts, tok_dev, width), BF16),
            pltpu.VMEM((CHUNKS, n_z, depth, 2 * fc), BF16),
            pltpu.VMEM((CHUNKS, n_z, fc, depth), BF16),
            pltpu.VMEM((CHUNKS, n_z, depth, 2 * fc), BF16),
            pltpu.VMEM((CHUNKS, n_z, fc, depth), BF16),
            pltpu.VMEM((CHUNKS, 2, hops, depth, 2 * fc), BF16),
            pltpu.VMEM((CHUNKS, 2, hops, fc, depth), BF16),
            pltpu.VMEM((experts, tok_dev, width), F32),
            pltpu.VMEM((experts, tok_dev, 2 * fc), BF16),
            pltpu.VMEM((experts, tok_dev, fc), BF16),
            pltpu.VMEM((4, tok_dev, width), BF16),
            pltpu.VMEM((4, tok_dev, width), BF16),
            pltpu.VMEM((4, 2, tok_dev // 2, width), BF16),
            pltpu.VMEM((2, tok_dev // 2, width), BF16),
            pltpu.VMEM((2, 2, tok_dev // 2, width), BF16),
            dma((3 + 3 * CHUNKS,)),
            dma((CHUNKS, 2, hops, 2)),
            dma((CHUNKS, 2, hops, 2)),
            dma((CHUNKS, 2, hops, 2)),
            dma((CHUNKS, 2, hops, 2)),
            dma((8,)),
            dma((8,)),
            dma((10,)),
            dma((10,)),
        ],
        compiler_params=pltpu.CompilerParams(
            collective_id=0, has_side_effects=True, vmem_limit_bytes=63 * 1024 * 1024
        ),
    )(tokens, cotangent, gates, w_gate[0], w_up[0], w_down[0])
    return token_grad, gate_grad[None], up_grad[None], down_grad[None]


def place_slots(routes, experts, capacity):
    expert_ids = routes.reshape(-1)
    onehot = (expert_ids[:, None] == jnp.arange(experts, dtype=jnp.int32)[None, :]).astype(
        jnp.int32
    )
    before = jnp.cumsum(onehot, axis=0) - onehot
    slot = jnp.sum(before * onehot, axis=1)
    return expert_ids * capacity + slot


def forward_part(x_rows, weight_gate, weight_up):
    gate_pre = jnp.dot(x_rows, weight_gate, preferred_element_type=jnp.float32)
    up_pre = jnp.dot(x_rows, weight_up, preferred_element_type=jnp.float32)
    sigmoid_gate = 1.0 / (1.0 + jnp.exp(-gate_pre))
    activated = gate_pre * sigmoid_gate
    hidden = (activated * up_pre).astype(jnp.bfloat16)
    return (gate_pre, up_pre, sigmoid_gate, activated, hidden)


def exchanged(tokens, cotangent, routes, gate_values, w_gate, w_up, w_down):
    experts = lax.axis_size("expert")
    tok_dev, model_width = tokens.shape
    fan_out = routes.shape[1]
    capacity = min(tok_dev, 3 * tok_dev * fan_out // (2 * experts))
    slot_index = place_slots(routes, experts, capacity)
    source_tok = jnp.arange(tok_dev * fan_out, dtype=jnp.int32) // fan_out

    def pack_rows(values):
        buffer = (
            jnp.zeros((experts * capacity, model_width), values.dtype)
            .at[slot_index]
            .set(values[source_tok])
        )
        return buffer.reshape(experts, capacity, model_width)

    gate_slots = (
        jnp.zeros((experts * capacity,), gate_values.dtype)
        .at[slot_index]
        .set(gate_values.reshape(-1))
    )
    gate_slots = gate_slots.reshape(experts, capacity)
    full_gate, full_up, full_down = (
        lax.all_gather(w_gate, "dp", axis=1, tiled=True),
        lax.all_gather(w_up, "dp", axis=1, tiled=True),
        lax.all_gather(w_down, "dp", axis=2, tiled=True),
    )
    full_gate = full_gate[0]
    full_up = full_up[0]
    recv_x, recv_dy, recv_gate = (
        lax.all_to_all(pack_rows(tokens), "expert", split_axis=0, concat_axis=0, tiled=True),
        lax.all_to_all(pack_rows(cotangent), "expert", split_axis=0, concat_axis=0, tiled=True),
        lax.all_to_all(gate_slots, "expert", split_axis=0, concat_axis=0, tiled=True),
    )
    x_rows = recv_x.reshape(-1, model_width)
    gate_pre, up_pre, sigmoid_gate, activated, hidden = forward_part(x_rows, full_gate, full_up)
    dy_rows = recv_dy.reshape(-1, model_width)
    scaled = (recv_gate.reshape(-1, 1).astype(jnp.float32) * dy_rows.astype(jnp.float32)).astype(
        jnp.bfloat16
    )
    hidden_grad = lax.dot_general(
        scaled, full_down[0], (((1,), (1,)), ((), ())), preferred_element_type=jnp.float32
    )
    down_term = lax.dot_general(
        hidden, scaled, (((0,), (0,)), ((), ())), preferred_element_type=jnp.float32
    )
    gate_grad = (
        hidden_grad * up_pre * sigmoid_gate * (1.0 + gate_pre * (1.0 - sigmoid_gate))
    ).astype(jnp.bfloat16)
    up_grad = (hidden_grad * activated).astype(jnp.bfloat16)
    row_grad = lax.dot_general(
        gate_grad, full_gate, (((1,), (1,)), ((), ())), preferred_element_type=jnp.float32
    )
    row_grad = row_grad + lax.dot_general(
        up_grad, full_up, (((1,), (1,)), ((), ())), preferred_element_type=jnp.float32
    )
    returned = lax.all_to_all(
        row_grad.astype(jnp.bfloat16).reshape(experts, capacity, model_width),
        "expert",
        split_axis=0,
        concat_axis=0,
        tiled=True,
    )
    picked = returned.reshape(experts * capacity, model_width)[slot_index]
    token_grad = jnp.sum(
        picked.astype(jnp.float32).reshape(tok_dev, fan_out, model_width), axis=1
    ).astype(jnp.bfloat16)
    gate_term = lax.dot_general(
        x_rows, gate_grad, (((0,), (0,)), ((), ())), preferred_element_type=jnp.float32
    )
    up_term = lax.dot_general(
        x_rows, up_grad, (((0,), (0,)), ((), ())), preferred_element_type=jnp.float32
    )
    gate_sum, up_sum, down_sum = (
        lax.psum_scatter(
            gate_term[None].astype(jnp.bfloat16), "dp", scatter_dimension=1, tiled=True
        ).astype(jnp.float32),
        lax.psum_scatter(
            up_term[None].astype(jnp.bfloat16), "dp", scatter_dimension=1, tiled=True
        ).astype(jnp.float32),
        lax.psum_scatter(
            down_term[None].astype(jnp.bfloat16), "dp", scatter_dimension=2, tiled=True
        ).astype(jnp.float32),
    )
    return (
        token_grad,
        gate_sum.astype(jnp.bfloat16),
        up_sum.astype(jnp.bfloat16),
        down_sum.astype(jnp.bfloat16),
    )


def solution(mesh):
    in_specs = (
        P(("expert", "dp"), None),
        P(("expert", "dp"), None),
        P(("expert", "dp"), None),
        P(("expert", "dp"), None),
        P("expert", "dp", None),
        P("expert", "dp", None),
        P("expert", None, "dp"),
    )
    out_specs = (
        P(("expert", "dp"), None),
        P("expert", "dp", None),
        P("expert", "dp", None),
        P("expert", None, "dp"),
    )
    small = mesh.shape["expert"] == 8 and mesh.shape["dp"] == 4
    local = one_kernel if small else exchanged
    return jax.shard_map(local, mesh=mesh, in_specs=in_specs, out_specs=out_specs, check_vma=False)
```

```python
import jax
import jax.numpy as jnp
from jax import lax
from jax.experimental import pallas as pl
from jax.experimental.pallas import tpu as pltpu
from jax.sharding import PartitionSpec as P

MESH = pl.DeviceIdType.MESH
BF16 = jnp.bfloat16
F32 = jnp.float32
CHUNKS = 4
GATE_LANES = 128


def contract(left, right, dims):
    return lax.dot_general(left, right, ((dims[:1], dims[1:]), ((), ())), preferred_element_type=F32)


def moe_kernel(
    tok_in, cot_in, gate_in, wg_in, wu_in, wd_in,
    tok_out, gg_out, gu_out, gd_out,
    rows, scaled, w1, w2, parts, sums, total, gu, turned,
    pair_send, pair_recv, chip_sum, diag_recv, near_recv,
    load_sem, ag_send, ag_recv, rs_send, rs_recv, tok_send, tok_recv, ret_send, ret_recv,
):
    e, z = lax.axis_index("expert"), lax.axis_index("dp")
    n_dev, tok_dev, width = scaled.shape
    chunks, n_z, depth, fc2 = w1.shape
    fc = fc2 // 2
    last = n_z - 1
    core, x, y = e % 2, (e // 2) % 2, e // 4
    partner = e + 1 - 2 * core
    near_x = e + 2 - 4 * x
    near_y = e + 4 - 8 * y
    diag = near_x + 4 - 8 * y
    half = tok_dev // 2

    loads = [
        pltpu.make_async_copy(tok_in, rows.at[e, :, pl.ds(0, width)], load_sem.at[0]),
        pltpu.make_async_copy(cot_in, rows.at[e, :, pl.ds(width, width)], load_sem.at[1]),
        pltpu.make_async_copy(gate_in, rows.at[e, :, pl.ds(2 * width, GATE_LANES)], load_sem.at[2]),
    ]
    for f in range(chunks):
        cols = pl.ds(f * fc, fc)
        k = 3 + 3 * f
        loads += [
            pltpu.make_async_copy(wg_in.at[:, cols], w1.at[f, z, :, pl.ds(0, fc)], load_sem.at[k]),
            pltpu.make_async_copy(wu_in.at[:, cols], w1.at[f, z, :, pl.ds(fc, fc)], load_sem.at[k + 1]),
            pltpu.make_async_copy(wd_in.at[cols, :], w2.at[f, z], load_sem.at[k + 2]),
        ]
    for load in loads:
        load.start()

    barrier = pltpu.get_barrier_semaphore()
    for near in (partner, near_x, near_y):
        pl.semaphore_signal(barrier, inc=1, device_id=(near, z), device_id_type=MESH)

    @pl.when(z > 0)
    def _():
        pl.semaphore_signal(barrier, inc=1, device_id=(e, z - 1), device_id_type=MESH)

    @pl.when(z < last)
    def _():
        pl.semaphore_signal(barrier, inc=1, device_id=(e, z + 1), device_id_type=MESH)

    for load in loads:
        load.wait()
    pl.semaphore_wait(barrier, 3 + jnp.minimum(z, 1) + jnp.minimum(last - z, 1))

    def remote(src, dst, send, recv, target):
        return pltpu.make_async_remote_copy(
            src_ref=src, dst_ref=dst, send_sem=send, recv_sem=recv, device_id=target, device_id_type=MESH
        )

    def ag_pair(f, way, s, block):
        target = (e, z + 1) if way == 0 else (e, z - 1)
        return [
            remote(w.at[f, block], w.at[f, block], ag_send.at[f, way, s, i], ag_recv.at[f, way, s, i], target)
            for i, w in enumerate((w1, w2))
        ]

    def ag_sends(f, way, s):
        ok = (z >= s) & (z < last) if way == 0 else (z + s <= last) & (z > 0)
        block = jnp.clip(z - s if way == 0 else z + s, 0, last)
        return ok, ag_pair(f, way, s, block)

    def ag_start(f, s):
        for way in range(2):
            ok, copies = ag_sends(f, way, s)

            @pl.when(ok)
            def _():
                for copy in copies:
                    copy.start()

    def ag_wait(f, s):
        for way in range(2):
            block = z - 1 - s if way == 0 else z + 1 + s
            ok = block >= 0 if way == 0 else block <= last
            copies = ag_pair(f, way, s, jnp.clip(block, 0, last))

            @pl.when(ok)
            def _():
                for copy in copies:
                    copy.wait_recv()

    def rs_pair(f, way, s, block):
        target = (e, z + 1) if way == 0 else (e, z - 1)
        return [remote(parts.at[f, block], sums.at[f, way, s], rs_send.at[f, way, s], rs_recv.at[f, way, s], target)]

    def rs_place(way, s):
        place = z if way == 0 else last - z
        block = jnp.clip(last + z - s if way == 0 else s + z - last, 0, last)
        return place, block

    def add_in(dst, src):
        step = 64

        @pl.loop(0, dst.shape[0] // step)
        def _(i):
            at = pl.ds(pl.multiple_of(i * step, step), step)
            dst[at, :] = (dst[at, :].astype(F32) + src[at, :].astype(F32)).astype(BF16)

    def rs_take(f, way, s, block):
        for copy in rs_pair(f, way, s, block):
            copy.wait_recv()
        add_in(parts.at[f, block], sums.at[f, way, s])

    def rs_slot(f, s, also):
        for way in range(2):
            place, block = rs_place(way, s)
            if s > 0:

                @pl.when(also & (s >= place) & (place > 0))
                def _():
                    rs_take(f, way, s - 1, block)

            @pl.when(also & (s >= place))
            def _():
                for copy in rs_pair(f, way, s, block):
                    copy.start()

    def rs_end(f):
        for way in range(2):
            place, _block = rs_place(way, 0)

            @pl.when(place > 0)
            def _():
                rs_take(f, way, last - 1, z)

    lo, hi = pl.ds(0, half), pl.ds(half, half)

    def rows_copy(block, k, target, part=None):
        ref = rows.at[block] if part is None else rows.at[block, part]
        return remote(ref, ref, tok_send.at[k], tok_recv.at[k], (target, z))

    flip = 1 - 2 * core
    own_sends = [rows_copy(e, 0, near_x), rows_copy(e, 1, near_y), rows_copy(e, 4, partner)]
    first_recv = [rows_copy(near_x, 0, near_x), rows_copy(near_y, 1, near_y)]
    second_sends = [
        rows_copy(near_x, 2, near_y, lo), rows_copy(near_y, 3, near_x, hi),
        rows_copy(near_x, 5, partner), rows_copy(near_y, 6, partner),
    ]
    second_recv = [rows_copy(diag, 2, near_y, lo), rows_copy(diag, 3, near_x, hi)]
    third_sends = [rows_copy(diag, 7, partner)]
    third_recv = [
        rows_copy(partner, 4, partner), rows_copy(near_x + flip, 5, partner),
        rows_copy(near_y + flip, 6, partner), rows_copy(diag + flip, 7, partner),
    ]

    def scale_block(d, carry):
        lanes = lax.broadcasted_iota(jnp.int32, (tok_dev, GATE_LANES), 1)
        gates = rows[d, :, 2 * width : 2 * width + GATE_LANES].astype(F32)
        gate = jnp.sum(jnp.where(lanes == e, gates, 0.0), axis=1, keepdims=True)
        scaled[d] = (gate * rows[d, :, width : 2 * width].astype(F32)).astype(BF16)
        return carry

    def forward_tile(f, i):
        at = pl.ds(2 * i, 2)
        tile = 2 * tok_dev
        x_rows = rows[at, :, 0:width].reshape(tile, width)
        pre = jnp.dot(x_rows, w1[f].reshape(width, fc2), preferred_element_type=F32)
        hidden_grad = jnp.zeros((tile, fc), F32)
        for b in range(n_z):
            dy = scaled[at, :, b * depth : (b + 1) * depth].reshape(tile, depth)
            hidden_grad += contract(dy, w2[f, b], (1, 1))
        gate_pre, up_pre = pre[:, :fc], pre[:, fc:]
        sig = 1.0 / (1.0 + jnp.exp(-gate_pre))
        act = gate_pre * sig
        hidden = (act * up_pre).astype(BF16)
        gate_grad = (hidden_grad * up_pre * sig * (1.0 + gate_pre * (1.0 - sig))).astype(BF16)
        up_grad = (hidden_grad * act).astype(BF16)
        gu[at, :, 0:fc] = gate_grad.reshape(2, tok_dev, fc)
        gu[at, :, fc:fc2] = up_grad.reshape(2, tok_dev, fc)
        lanes = pl.ds(pl.multiple_of(i * tile, tile), tile)
        for k, value in enumerate((gate_grad, up_grad, hidden)):
            turned[k * fc : (k + 1) * fc, lanes] = value.T

    def weight_grads(f):
        all_rows = n_dev * tok_dev
        for b in range(n_z):
            cut = slice(b * depth, (b + 1) * depth)
            x_cut = rows[:, :, cut].reshape(all_rows, depth)
            parts[f, b, 0:fc2, :] = jnp.dot(turned[0:fc2, :], x_cut, preferred_element_type=F32).astype(BF16)
            dy_cut = scaled[:, :, cut].reshape(all_rows, depth)
            parts[f, b, fc2:, :] = jnp.dot(turned[fc2:, :], dy_cut, preferred_element_type=F32).astype(BF16)

    def row_tile(f, i):
        at = pl.ds(2 * i, 2)
        left = gu[at].reshape(2 * tok_dev, fc2)
        for b in range(n_z):
            part = contract(left, w1[f, b], (1, 1)).reshape(2, tok_dev, depth)
            cut = slice(b * depth, (b + 1) * depth)

            @pl.when(f == 0)
            def _():
                total[at, :, cut] = part

            @pl.when(f > 0)
            def _():
                total[at, :, cut] = total[at, :, cut] + part

    ag_start(0, 0)
    for copy in own_sends:
        copy.start()
    ag_wait(0, 0)
    ag_start(0, 1)
    for i in range(2):
        first_recv[i].wait_recv()
        second_sends[i].start()
        second_sends[i + 2].start()
    ag_wait(0, 1)
    ag_start(0, 2)
    ag_start(1, 0)
    for copy in second_recv:
        copy.wait_recv()
    third_sends[0].start()
    for copy in third_recv:
        copy.wait_recv()
    lax.fori_loop(0, n_dev, scale_block, 0)
    ag_wait(0, 2)

    tiles = n_dev // 2

    @pl.loop(0, chunks)
    def _(f):
        before, after = jnp.maximum(f - 1, 0), jnp.minimum(f + 1, chunks - 1)
        more = f + 1 < chunks

        def hop(s):
            @pl.when(more)
            def _():
                ag_wait(after, s)
                if s < 2:
                    ag_start(after, s + 1)

            if s == 1:

                @pl.when(f + 2 < chunks)
                def _():
                    ag_start(jnp.minimum(f + 2, chunks - 1), 0)

        @pl.loop(0, tiles // 2)
        def _(i):
            forward_tile(f, i)

        hop(0)
        rs_slot(before, 1, f > 0)

        @pl.loop(tiles // 2, tiles)
        def _(i):
            forward_tile(f, i)

        hop(1)
        rs_slot(before, 2, f > 0)
        weight_grads(f)
        rs_slot(f, 0, f >= 0)

        @pl.loop(0, tiles)
        def _(i):
            row_tile(f, i)

        hop(2)

        @pl.when(f > 0)
        def _():
            rs_end(before)

    final = chunks - 1
    places = [(e, partner), (near_x, near_x + flip), (near_y, near_y + flip), (diag, diag + flip)]

    def pair_copy(k):
        return remote(pair_send.at[k], pair_recv.at[k], ret_send.at[k], ret_recv.at[k], (partner, z))

    for k in (3, 1, 2, 0):
        pair_send[k] = total[places[k][1]].astype(BF16)
        pair_copy(k).start()
    rs_slot(final, 1, final >= 0)
    for k in (3, 1, 2, 0):
        pair_copy(k).wait_recv()
        chip_sum[k] = (total[places[k][0]] + pair_recv[k].astype(F32)).astype(BF16).reshape(2, half, width)
        if k == 3:
            diag_copies = [
                remote(chip_sum.at[3, 0], diag_recv.at[0], ret_send.at[4], ret_recv.at[4], (near_x, z)),
                remote(chip_sum.at[3, 1], diag_recv.at[1], ret_send.at[5], ret_recv.at[5], (near_y, z)),
            ]
            for copy in diag_copies:
                copy.start()
    near_copies = [
        remote(chip_sum.at[1, 0], near_recv.at[0, 0], ret_send.at[6], ret_recv.at[6], (near_x, z)),
        remote(chip_sum.at[2, 1], near_recv.at[1, 1], ret_send.at[7], ret_recv.at[7], (near_y, z)),
        remote(chip_sum.at[2, 0], near_recv.at[1, 0], ret_send.at[8], ret_recv.at[8], (near_y, z)),
        remote(chip_sum.at[1, 1], near_recv.at[0, 1], ret_send.at[9], ret_recv.at[9], (near_x, z)),
    ]
    near_copies[0].start()
    near_copies[1].start()
    diag_copies[0].wait_recv()
    add_in(chip_sum.at[2, 0], diag_recv.at[0])
    near_copies[2].start()
    diag_copies[1].wait_recv()
    add_in(chip_sum.at[1, 1], diag_recv.at[1])
    near_copies[3].start()
    for s in range(2, n_z - 1):
        rs_slot(final, s, final >= 0)
    for copy in near_copies:
        copy.wait_recv()
    for h in range(2):
        tok_out[h * half : (h + 1) * half, :] = (
            chip_sum[0, h].astype(F32) + near_recv[0, h].astype(F32) + near_recv[1, h].astype(F32)
        ).astype(BF16)
    rs_end(final)
    for f in range(chunks):
        cols = slice(f * fc, (f + 1) * fc)
        gg_out[:, cols] = parts[f, z, 0:fc, :].T
        gu_out[:, cols] = parts[f, z, fc:fc2, :].T
        gd_out[cols, :] = parts[f, z, fc2:, :]

    @pl.loop(0, chunks)
    def _(f):
        for way in range(2):
            for s in range(n_z - 1):
                ok, copies = ag_sends(f, way, s)

                @pl.when(ok)
                def _():
                    for copy in copies:
                        copy.wait_send()

                place, block = rs_place(way, s)

                @pl.when(s >= place)
                def _():
                    for copy in rs_pair(f, way, s, block):
                        copy.wait_send()

    for copy in own_sends + second_sends + third_sends + diag_copies + near_copies:
        copy.wait_send()
    for k in range(4):
        pair_copy(k).wait_send()


def one_kernel(tokens, cotangent, routes, gate_values, w_gate, w_up, w_down):
    experts, n_z = lax.axis_size("expert"), lax.axis_size("dp")
    tok_dev, width = tokens.shape
    depth, ff = w_gate.shape[1:]
    fc = ff // CHUNKS
    lanes = jnp.arange(GATE_LANES, dtype=jnp.int32)
    named = routes[:, :, None] == lanes[None, None, :]
    gates = jnp.sum(jnp.where(named, gate_values[:, :, None].astype(F32), 0.0), axis=1).astype(BF16)
    dma = pltpu.SemaphoreType.DMA
    hops = n_z - 1
    any_spec, vmem_spec = pl.BlockSpec(memory_space=pl.ANY), pl.BlockSpec(memory_space=pltpu.VMEM)
    token_grad, gate_grad, up_grad, down_grad = pl.pallas_call(
        moe_kernel,
        out_shape=(
            jax.ShapeDtypeStruct((tok_dev, width), BF16),
            jax.ShapeDtypeStruct((depth, ff), BF16),
            jax.ShapeDtypeStruct((depth, ff), BF16),
            jax.ShapeDtypeStruct((ff, depth), BF16),
        ),
        in_specs=[any_spec] * 6,
        out_specs=(vmem_spec,) * 4,
        scratch_shapes=[
            pltpu.VMEM((experts, tok_dev, 2 * width + GATE_LANES), BF16),
            pltpu.VMEM((experts, tok_dev, width), BF16),
            pltpu.VMEM((CHUNKS, n_z, depth, 2 * fc), BF16),
            pltpu.VMEM((CHUNKS, n_z, fc, depth), BF16),
            pltpu.VMEM((CHUNKS, n_z, 3 * fc, depth), BF16),
            pltpu.VMEM((CHUNKS, 2, hops, 3 * fc, depth), BF16),
            pltpu.VMEM((experts, tok_dev, width), F32),
            pltpu.VMEM((experts, tok_dev, 2 * fc), BF16),
            pltpu.VMEM((3 * fc, experts * tok_dev), BF16),
            pltpu.VMEM((4, tok_dev, width), BF16),
            pltpu.VMEM((4, tok_dev, width), BF16),
            pltpu.VMEM((4, 2, tok_dev // 2, width), BF16),
            pltpu.VMEM((2, tok_dev // 2, width), BF16),
            pltpu.VMEM((2, 2, tok_dev // 2, width), BF16),
            dma((3 + 3 * CHUNKS,)),
            dma((CHUNKS, 2, hops, 2)),
            dma((CHUNKS, 2, hops, 2)),
            dma((CHUNKS, 2, hops)),
            dma((CHUNKS, 2, hops)),
            dma((8,)),
            dma((8,)),
            dma((10,)),
            dma((10,)),
        ],
        compiler_params=pltpu.CompilerParams(
            collective_id=0, has_side_effects=True, vmem_limit_bytes=63 * 1024 * 1024
        ),
    )(tokens, cotangent, gates, w_gate[0], w_up[0], w_down[0])
    return token_grad, gate_grad[None], up_grad[None], down_grad[None]


def place_slots(routes, experts, capacity):
    expert_ids = routes.reshape(-1)
    onehot = (expert_ids[:, None] == jnp.arange(experts, dtype=jnp.int32)[None, :]).astype(
        jnp.int32
    )
    before = jnp.cumsum(onehot, axis=0) - onehot
    slot = jnp.sum(before * onehot, axis=1)
    return expert_ids * capacity + slot


def forward_part(x_rows, weight_gate, weight_up):
    gate_pre = jnp.dot(x_rows, weight_gate, preferred_element_type=jnp.float32)
    up_pre = jnp.dot(x_rows, weight_up, preferred_element_type=jnp.float32)
    sigmoid_gate = 1.0 / (1.0 + jnp.exp(-gate_pre))
    activated = gate_pre * sigmoid_gate
    hidden = (activated * up_pre).astype(jnp.bfloat16)
    return (gate_pre, up_pre, sigmoid_gate, activated, hidden)


def exchanged(tokens, cotangent, routes, gate_values, w_gate, w_up, w_down):
    experts = lax.axis_size("expert")
    tok_dev, model_width = tokens.shape
    fan_out = routes.shape[1]
    capacity = min(tok_dev, 3 * tok_dev * fan_out // (2 * experts))
    slot_index = place_slots(routes, experts, capacity)
    source_tok = jnp.arange(tok_dev * fan_out, dtype=jnp.int32) // fan_out

    def pack_rows(values):
        buffer = (
            jnp.zeros((experts * capacity, model_width), values.dtype)
            .at[slot_index]
            .set(values[source_tok])
        )
        return buffer.reshape(experts, capacity, model_width)

    gate_slots = (
        jnp.zeros((experts * capacity,), gate_values.dtype)
        .at[slot_index]
        .set(gate_values.reshape(-1))
    )
    gate_slots = gate_slots.reshape(experts, capacity)
    full_gate, full_up, full_down = (
        lax.all_gather(w_gate, "dp", axis=1, tiled=True),
        lax.all_gather(w_up, "dp", axis=1, tiled=True),
        lax.all_gather(w_down, "dp", axis=2, tiled=True),
    )
    full_gate = full_gate[0]
    full_up = full_up[0]
    recv_x, recv_dy, recv_gate = (
        lax.all_to_all(pack_rows(tokens), "expert", split_axis=0, concat_axis=0, tiled=True),
        lax.all_to_all(pack_rows(cotangent), "expert", split_axis=0, concat_axis=0, tiled=True),
        lax.all_to_all(gate_slots, "expert", split_axis=0, concat_axis=0, tiled=True),
    )
    x_rows = recv_x.reshape(-1, model_width)
    gate_pre, up_pre, sigmoid_gate, activated, hidden = forward_part(x_rows, full_gate, full_up)
    dy_rows = recv_dy.reshape(-1, model_width)
    scaled = (recv_gate.reshape(-1, 1).astype(jnp.float32) * dy_rows.astype(jnp.float32)).astype(
        jnp.bfloat16
    )
    hidden_grad = lax.dot_general(
        scaled, full_down[0], (((1,), (1,)), ((), ())), preferred_element_type=jnp.float32
    )
    down_term = lax.dot_general(
        hidden, scaled, (((0,), (0,)), ((), ())), preferred_element_type=jnp.float32
    )
    gate_grad = (
        hidden_grad * up_pre * sigmoid_gate * (1.0 + gate_pre * (1.0 - sigmoid_gate))
    ).astype(jnp.bfloat16)
    up_grad = (hidden_grad * activated).astype(jnp.bfloat16)
    row_grad = lax.dot_general(
        gate_grad, full_gate, (((1,), (1,)), ((), ())), preferred_element_type=jnp.float32
    )
    row_grad = row_grad + lax.dot_general(
        up_grad, full_up, (((1,), (1,)), ((), ())), preferred_element_type=jnp.float32
    )
    returned = lax.all_to_all(
        row_grad.astype(jnp.bfloat16).reshape(experts, capacity, model_width),
        "expert",
        split_axis=0,
        concat_axis=0,
        tiled=True,
    )
    picked = returned.reshape(experts * capacity, model_width)[slot_index]
    token_grad = jnp.sum(
        picked.astype(jnp.float32).reshape(tok_dev, fan_out, model_width), axis=1
    ).astype(jnp.bfloat16)
    gate_term = lax.dot_general(
        x_rows, gate_grad, (((0,), (0,)), ((), ())), preferred_element_type=jnp.float32
    )
    up_term = lax.dot_general(
        x_rows, up_grad, (((0,), (0,)), ((), ())), preferred_element_type=jnp.float32
    )
    gate_sum, up_sum, down_sum = (
        lax.psum_scatter(
            gate_term[None].astype(jnp.bfloat16), "dp", scatter_dimension=1, tiled=True
        ).astype(jnp.float32),
        lax.psum_scatter(
            up_term[None].astype(jnp.bfloat16), "dp", scatter_dimension=1, tiled=True
        ).astype(jnp.float32),
        lax.psum_scatter(
            down_term[None].astype(jnp.bfloat16), "dp", scatter_dimension=2, tiled=True
        ).astype(jnp.float32),
    )
    return (
        token_grad,
        gate_sum.astype(jnp.bfloat16),
        up_sum.astype(jnp.bfloat16),
        down_sum.astype(jnp.bfloat16),
    )


def solution(mesh):
    in_specs = (
        P(("expert", "dp"), None),
        P(("expert", "dp"), None),
        P(("expert", "dp"), None),
        P(("expert", "dp"), None),
        P("expert", "dp", None),
        P("expert", "dp", None),
        P("expert", None, "dp"),
    )
    out_specs = (
        P(("expert", "dp"), None),
        P("expert", "dp", None),
        P("expert", "dp", None),
        P("expert", None, "dp"),
    )
    small = mesh.shape["expert"] == 8 and mesh.shape["dp"] == 4
    local = one_kernel if small else exchanged
    return jax.shard_map(local, mesh=mesh, in_specs=in_specs, out_specs=out_specs, check_vma=False)
```

```python
import jax
import jax.numpy as jnp
from jax import lax
from jax.experimental import pallas as pl
from jax.experimental.pallas import tpu as pltpu
from jax.sharding import PartitionSpec as P

MESH = pl.DeviceIdType.MESH
BF16 = jnp.bfloat16
F32 = jnp.float32
CHUNKS = 4
GATE_LANES = 128


def contract(left, right, dims):
    return lax.dot_general(left, right, ((dims[:1], dims[1:]), ((), ())), preferred_element_type=F32)


def moe_kernel(
    tok_in, cot_in, gate_in, wg_in, wu_in, wd_in,
    tok_out, gg_out, gu_out, gd_out,
    rows, scaled, w1, w2, parts, sums, total, gu, turned,
    pair_send, pair_recv, chip_sum, diag_recv, near_recv,
    load_sem, ag_send, ag_recv, rs_send, rs_recv, tok_send, tok_recv, ret_send, ret_recv,
):
    e, z = lax.axis_index("expert"), lax.axis_index("dp")
    n_dev, tok_dev, width = scaled.shape
    chunks, n_z, depth, fc2 = w1.shape
    fc = fc2 // 2
    last = n_z - 1
    core, x, y = e % 2, (e // 2) % 2, e // 4
    partner = e + 1 - 2 * core
    near_x = e + 2 - 4 * x
    near_y = e + 4 - 8 * y
    diag = near_x + 4 - 8 * y
    half = tok_dev // 2

    loads = [
        pltpu.make_async_copy(tok_in, rows.at[e, :, pl.ds(0, width)], load_sem.at[0]),
        pltpu.make_async_copy(cot_in, rows.at[e, :, pl.ds(width, width)], load_sem.at[1]),
        pltpu.make_async_copy(gate_in, rows.at[e, :, pl.ds(2 * width, GATE_LANES)], load_sem.at[2]),
    ]
    for f in range(chunks):
        cols = pl.ds(f * fc, fc)
        k = 3 + 3 * f
        loads += [
            pltpu.make_async_copy(wg_in.at[:, cols], w1.at[f, z, :, pl.ds(0, fc)], load_sem.at[k]),
            pltpu.make_async_copy(wu_in.at[:, cols], w1.at[f, z, :, pl.ds(fc, fc)], load_sem.at[k + 1]),
            pltpu.make_async_copy(wd_in.at[cols, :], w2.at[f, z], load_sem.at[k + 2]),
        ]
    for load in loads:
        load.start()

    barrier = pltpu.get_barrier_semaphore()
    for near in (partner, near_x, near_y):
        pl.semaphore_signal(barrier, inc=1, device_id=(near, z), device_id_type=MESH)

    @pl.when(z > 0)
    def _():
        pl.semaphore_signal(barrier, inc=1, device_id=(e, z - 1), device_id_type=MESH)

    @pl.when(z < last)
    def _():
        pl.semaphore_signal(barrier, inc=1, device_id=(e, z + 1), device_id_type=MESH)

    for load in loads:
        load.wait()
    pl.semaphore_wait(barrier, 3 + jnp.minimum(z, 1) + jnp.minimum(last - z, 1))

    def remote(src, dst, send, recv, target):
        return pltpu.make_async_remote_copy(
            src_ref=src, dst_ref=dst, send_sem=send, recv_sem=recv, device_id=target, device_id_type=MESH
        )

    def ag_pair(f, way, s, block):
        target = (e, z + 1) if way == 0 else (e, z - 1)
        return [
            remote(w.at[f, block], w.at[f, block], ag_send.at[f, way, s, i], ag_recv.at[f, way, s, i], target)
            for i, w in enumerate((w1, w2))
        ]

    def ag_sends(f, way, s):
        ok = (z >= s) & (z < last) if way == 0 else (z + s <= last) & (z > 0)
        block = jnp.clip(z - s if way == 0 else z + s, 0, last)
        return ok, ag_pair(f, way, s, block)

    def ag_start(f, s):
        for way in range(2):
            ok, copies = ag_sends(f, way, s)

            @pl.when(ok)
            def _():
                for copy in copies:
                    copy.start()

    def ag_hop(f, s):
        for i in range(2):
            for way in range(2):
                block = z - 1 - s if way == 0 else z + 1 + s
                here = block >= 0 if way == 0 else block <= last
                arriving = ag_pair(f, way, s, jnp.clip(block, 0, last))[i]

                @pl.when(here)
                def _():
                    arriving.wait_recv()

                if s < n_z - 2:
                    ok, copies = ag_sends(f, way, s + 1)

                    @pl.when(ok)
                    def _():
                        copies[i].start()

    def rs_pair(f, way, s, block):
        target = (e, z + 1) if way == 0 else (e, z - 1)
        piece = parts.shape[2] // 2
        return [
            remote(
                parts.at[f, block, pl.ds(i * piece, piece)], sums.at[f, way, s, pl.ds(i * piece, piece)],
                rs_send.at[f, way, s, i], rs_recv.at[f, way, s, i], target,
            )
            for i in range(2)
        ]

    def rs_place(way, s):
        place = z if way == 0 else last - z
        block = jnp.clip(last + z - s if way == 0 else s + z - last, 0, last)
        return place, block

    def add_in(dst, src):
        step = 64

        @pl.loop(0, dst.shape[0] // step)
        def _(i):
            at = pl.ds(pl.multiple_of(i * step, step), step)
            dst[at, :] = (dst[at, :].astype(F32) + src[at, :].astype(F32)).astype(BF16)

    def rs_take(f, way, s, block, i):
        piece = parts.shape[2] // 2
        rs_pair(f, way, s, block)[i].wait_recv()
        add_in(parts.at[f, block, pl.ds(i * piece, piece)], sums.at[f, way, s, pl.ds(i * piece, piece)])

    def rs_slot(f, s, also):
        for i in range(2):
            for way in range(2):
                place, block = rs_place(way, s)
                if s > 0:

                    @pl.when(also & (s >= place) & (place > 0))
                    def _():
                        rs_take(f, way, s - 1, block, i)

                @pl.when(also & (s >= place))
                def _():
                    rs_pair(f, way, s, block)[i].start()

    def rs_end(f):
        for way in range(2):
            place, _block = rs_place(way, 0)

            @pl.when(place > 0)
            def _():
                for i in range(2):
                    rs_take(f, way, last - 1, z, i)

    lo, hi = pl.ds(0, half), pl.ds(half, half)

    def rows_copy(block, k, target, part=None):
        ref = rows.at[block] if part is None else rows.at[block, part]
        return remote(ref, ref, tok_send.at[k], tok_recv.at[k], (target, z))

    flip = 1 - 2 * core
    own_sends = [rows_copy(e, 0, near_x), rows_copy(e, 1, near_y), rows_copy(e, 4, partner)]
    first_recv = [rows_copy(near_x, 0, near_x), rows_copy(near_y, 1, near_y)]
    second_sends = [
        rows_copy(near_x, 2, near_y, lo), rows_copy(near_y, 3, near_x, hi),
        rows_copy(near_x, 5, partner), rows_copy(near_y, 6, partner),
    ]
    second_recv = [rows_copy(diag, 2, near_y, lo), rows_copy(diag, 3, near_x, hi)]
    third_sends = [rows_copy(diag, 7, partner)]
    third_recv = [
        rows_copy(partner, 4, partner), rows_copy(near_x + flip, 5, partner),
        rows_copy(near_y + flip, 6, partner), rows_copy(diag + flip, 7, partner),
    ]

    def scale_block(d, carry):
        lanes = lax.broadcasted_iota(jnp.int32, (tok_dev, GATE_LANES), 1)
        gates = rows[d, :, 2 * width : 2 * width + GATE_LANES].astype(F32)
        gate = jnp.sum(jnp.where(lanes == e, gates, 0.0), axis=1, keepdims=True)
        scaled[d] = (gate * rows[d, :, width : 2 * width].astype(F32)).astype(BF16)
        return carry

    def forward_tile(f, i):
        at = pl.ds(2 * i, 2)
        tile = 2 * tok_dev
        x_rows = rows[at, :, 0:width].reshape(tile, width)
        pre = jnp.dot(x_rows, w1[f].reshape(width, fc2), preferred_element_type=F32)
        hidden_grad = jnp.zeros((tile, fc), F32)
        for b in range(n_z):
            dy = scaled[at, :, b * depth : (b + 1) * depth].reshape(tile, depth)
            hidden_grad += contract(dy, w2[f, b], (1, 1))
        gate_pre, up_pre = pre[:, :fc], pre[:, fc:]
        sig = 1.0 / (1.0 + jnp.exp(-gate_pre))
        act = gate_pre * sig
        hidden = (act * up_pre).astype(BF16)
        gate_grad = (hidden_grad * up_pre * sig * (1.0 + gate_pre * (1.0 - sig))).astype(BF16)
        up_grad = (hidden_grad * act).astype(BF16)
        gu[at, :, 0:fc] = gate_grad.reshape(2, tok_dev, fc)
        gu[at, :, fc:fc2] = up_grad.reshape(2, tok_dev, fc)
        lanes = pl.ds(pl.multiple_of(i * tile, tile), tile)
        for k, value in enumerate((gate_grad, up_grad, hidden)):
            turned[k * fc : (k + 1) * fc, lanes] = value.T

    def weight_grads(f):
        all_rows = n_dev * tok_dev
        for b in range(n_z):
            cut = slice(b * depth, (b + 1) * depth)
            x_cut = rows[:, :, cut].reshape(all_rows, depth)
            parts[f, b, 0:fc2, :] = jnp.dot(turned[0:fc2, :], x_cut, preferred_element_type=F32).astype(BF16)
            dy_cut = scaled[:, :, cut].reshape(all_rows, depth)
            parts[f, b, fc2:, :] = jnp.dot(turned[fc2:, :], dy_cut, preferred_element_type=F32).astype(BF16)

    def row_tile(f, i):
        at = pl.ds(2 * i, 2)
        left = gu[at].reshape(2 * tok_dev, fc2)
        for b in range(n_z):
            part = contract(left, w1[f, b], (1, 1)).reshape(2, tok_dev, depth)
            cut = slice(b * depth, (b + 1) * depth)

            @pl.when(f == 0)
            def _():
                total[at, :, cut] = part

            @pl.when(f > 0)
            def _():
                total[at, :, cut] = total[at, :, cut] + part

    ag_start(0, 0)
    for copy in own_sends:
        copy.start()
    ag_hop(0, 0)
    for i in range(2):
        first_recv[i].wait_recv()
        second_sends[i].start()
        second_sends[i + 2].start()
    ag_hop(0, 1)
    ag_start(1, 0)
    for copy in second_recv:
        copy.wait_recv()
    third_sends[0].start()
    for copy in third_recv:
        copy.wait_recv()
    lax.fori_loop(0, n_dev, scale_block, 0)
    ag_hop(0, 2)

    tiles = n_dev // 2

    @pl.loop(0, chunks)
    def _(f):
        before, after = jnp.maximum(f - 1, 0), jnp.minimum(f + 1, chunks - 1)
        more = f + 1 < chunks

        def hop(s):
            @pl.when(more)
            def _():
                ag_hop(after, s)

            if s == 1:

                @pl.when(f + 2 < chunks)
                def _():
                    ag_start(jnp.minimum(f + 2, chunks - 1), 0)

        @pl.loop(0, tiles // 2)
        def _(i):
            forward_tile(f, i)

        hop(0)
        rs_slot(before, 1, f > 0)

        @pl.loop(tiles // 2, tiles)
        def _(i):
            forward_tile(f, i)

        weight_grads(f)
        rs_slot(f, 0, f >= 0)
        hop(1)
        rs_slot(before, 2, f > 0)

        @pl.loop(0, tiles)
        def _(i):
            row_tile(f, i)

        hop(2)

        @pl.when(f > 0)
        def _():
            rs_end(before)

    final = chunks - 1
    places = [(e, partner), (near_x, near_x + flip), (near_y, near_y + flip), (diag, diag + flip)]

    def pair_copy(k):
        return remote(pair_send.at[k], pair_recv.at[k], ret_send.at[k], ret_recv.at[k], (partner, z))

    for k in (3, 1, 2, 0):
        pair_send[k] = total[places[k][1]].astype(BF16)
        pair_copy(k).start()
    rs_slot(final, 1, final >= 0)
    for k in (3, 1, 2, 0):
        pair_copy(k).wait_recv()
        chip_sum[k] = (total[places[k][0]] + pair_recv[k].astype(F32)).astype(BF16).reshape(2, half, width)
        if k == 3:
            diag_copies = [
                remote(chip_sum.at[3, 0], diag_recv.at[0], ret_send.at[4], ret_recv.at[4], (near_x, z)),
                remote(chip_sum.at[3, 1], diag_recv.at[1], ret_send.at[5], ret_recv.at[5], (near_y, z)),
            ]
            for copy in diag_copies:
                copy.start()
    near_copies = [
        remote(chip_sum.at[1, 0], near_recv.at[0, 0], ret_send.at[6], ret_recv.at[6], (near_x, z)),
        remote(chip_sum.at[2, 1], near_recv.at[1, 1], ret_send.at[7], ret_recv.at[7], (near_y, z)),
        remote(chip_sum.at[2, 0], near_recv.at[1, 0], ret_send.at[8], ret_recv.at[8], (near_y, z)),
        remote(chip_sum.at[1, 1], near_recv.at[0, 1], ret_send.at[9], ret_recv.at[9], (near_x, z)),
    ]
    near_copies[0].start()
    near_copies[1].start()
    diag_copies[0].wait_recv()
    add_in(chip_sum.at[2, 0], diag_recv.at[0])
    near_copies[2].start()
    diag_copies[1].wait_recv()
    add_in(chip_sum.at[1, 1], diag_recv.at[1])
    near_copies[3].start()
    for s in range(2, n_z - 1):
        rs_slot(final, s, final >= 0)
    for copy in near_copies:
        copy.wait_recv()
    for h in range(2):
        tok_out[h * half : (h + 1) * half, :] = (
            chip_sum[0, h].astype(F32) + near_recv[0, h].astype(F32) + near_recv[1, h].astype(F32)
        ).astype(BF16)
    rs_end(final)
    for f in range(chunks):
        cols = slice(f * fc, (f + 1) * fc)
        gg_out[:, cols] = parts[f, z, 0:fc, :].T
        gu_out[:, cols] = parts[f, z, fc:fc2, :].T
        gd_out[cols, :] = parts[f, z, fc2:, :]

    @pl.loop(0, chunks)
    def _(f):
        for way in range(2):
            for s in range(n_z - 1):
                ok, copies = ag_sends(f, way, s)

                @pl.when(ok)
                def _():
                    for copy in copies:
                        copy.wait_send()

                place, block = rs_place(way, s)

                @pl.when(s >= place)
                def _():
                    for copy in rs_pair(f, way, s, block):
                        copy.wait_send()

    for copy in own_sends + second_sends + third_sends + diag_copies + near_copies:
        copy.wait_send()
    for k in range(4):
        pair_copy(k).wait_send()


def one_kernel(tokens, cotangent, routes, gate_values, w_gate, w_up, w_down):
    experts, n_z = lax.axis_size("expert"), lax.axis_size("dp")
    tok_dev, width = tokens.shape
    depth, ff = w_gate.shape[1:]
    fc = ff // CHUNKS
    lanes = jnp.arange(GATE_LANES, dtype=jnp.int32)
    named = routes[:, :, None] == lanes[None, None, :]
    gates = jnp.sum(jnp.where(named, gate_values[:, :, None].astype(F32), 0.0), axis=1).astype(BF16)
    dma = pltpu.SemaphoreType.DMA
    hops = n_z - 1
    any_spec, vmem_spec = pl.BlockSpec(memory_space=pl.ANY), pl.BlockSpec(memory_space=pltpu.VMEM)
    token_grad, gate_grad, up_grad, down_grad = pl.pallas_call(
        moe_kernel,
        out_shape=(
            jax.ShapeDtypeStruct((tok_dev, width), BF16),
            jax.ShapeDtypeStruct((depth, ff), BF16),
            jax.ShapeDtypeStruct((depth, ff), BF16),
            jax.ShapeDtypeStruct((ff, depth), BF16),
        ),
        in_specs=[any_spec] * 6,
        out_specs=(vmem_spec,) * 4,
        scratch_shapes=[
            pltpu.VMEM((experts, tok_dev, 2 * width + GATE_LANES), BF16),
            pltpu.VMEM((experts, tok_dev, width), BF16),
            pltpu.VMEM((CHUNKS, n_z, depth, 2 * fc), BF16),
            pltpu.VMEM((CHUNKS, n_z, fc, depth), BF16),
            pltpu.VMEM((CHUNKS, n_z, 3 * fc, depth), BF16),
            pltpu.VMEM((CHUNKS, 2, hops, 3 * fc, depth), BF16),
            pltpu.VMEM((experts, tok_dev, width), F32),
            pltpu.VMEM((experts, tok_dev, 2 * fc), BF16),
            pltpu.VMEM((3 * fc, experts * tok_dev), BF16),
            pltpu.VMEM((4, tok_dev, width), BF16),
            pltpu.VMEM((4, tok_dev, width), BF16),
            pltpu.VMEM((4, 2, tok_dev // 2, width), BF16),
            pltpu.VMEM((2, tok_dev // 2, width), BF16),
            pltpu.VMEM((2, 2, tok_dev // 2, width), BF16),
            dma((3 + 3 * CHUNKS,)),
            dma((CHUNKS, 2, hops, 2)),
            dma((CHUNKS, 2, hops, 2)),
            dma((CHUNKS, 2, hops, 2)),
            dma((CHUNKS, 2, hops, 2)),
            dma((8,)),
            dma((8,)),
            dma((10,)),
            dma((10,)),
        ],
        compiler_params=pltpu.CompilerParams(
            collective_id=0, has_side_effects=True, vmem_limit_bytes=63 * 1024 * 1024
        ),
    )(tokens, cotangent, gates, w_gate[0], w_up[0], w_down[0])
    return token_grad, gate_grad[None], up_grad[None], down_grad[None]


def place_slots(routes, experts, capacity):
    expert_ids = routes.reshape(-1)
    onehot = (expert_ids[:, None] == jnp.arange(experts, dtype=jnp.int32)[None, :]).astype(
        jnp.int32
    )
    before = jnp.cumsum(onehot, axis=0) - onehot
    slot = jnp.sum(before * onehot, axis=1)
    return expert_ids * capacity + slot


def forward_part(x_rows, weight_gate, weight_up):
    gate_pre = jnp.dot(x_rows, weight_gate, preferred_element_type=jnp.float32)
    up_pre = jnp.dot(x_rows, weight_up, preferred_element_type=jnp.float32)
    sigmoid_gate = 1.0 / (1.0 + jnp.exp(-gate_pre))
    activated = gate_pre * sigmoid_gate
    hidden = (activated * up_pre).astype(jnp.bfloat16)
    return (gate_pre, up_pre, sigmoid_gate, activated, hidden)


def exchanged(tokens, cotangent, routes, gate_values, w_gate, w_up, w_down):
    experts = lax.axis_size("expert")
    tok_dev, model_width = tokens.shape
    fan_out = routes.shape[1]
    capacity = min(tok_dev, 3 * tok_dev * fan_out // (2 * experts))
    slot_index = place_slots(routes, experts, capacity)
    source_tok = jnp.arange(tok_dev * fan_out, dtype=jnp.int32) // fan_out

    def pack_rows(values):
        buffer = (
            jnp.zeros((experts * capacity, model_width), values.dtype)
            .at[slot_index]
            .set(values[source_tok])
        )
        return buffer.reshape(experts, capacity, model_width)

    gate_slots = (
        jnp.zeros((experts * capacity,), gate_values.dtype)
        .at[slot_index]
        .set(gate_values.reshape(-1))
    )
    gate_slots = gate_slots.reshape(experts, capacity)
    full_gate, full_up, full_down = (
        lax.all_gather(w_gate, "dp", axis=1, tiled=True),
        lax.all_gather(w_up, "dp", axis=1, tiled=True),
        lax.all_gather(w_down, "dp", axis=2, tiled=True),
    )
    full_gate = full_gate[0]
    full_up = full_up[0]
    recv_x, recv_dy, recv_gate = (
        lax.all_to_all(pack_rows(tokens), "expert", split_axis=0, concat_axis=0, tiled=True),
        lax.all_to_all(pack_rows(cotangent), "expert", split_axis=0, concat_axis=0, tiled=True),
        lax.all_to_all(gate_slots, "expert", split_axis=0, concat_axis=0, tiled=True),
    )
    x_rows = recv_x.reshape(-1, model_width)
    gate_pre, up_pre, sigmoid_gate, activated, hidden = forward_part(x_rows, full_gate, full_up)
    dy_rows = recv_dy.reshape(-1, model_width)
    scaled = (recv_gate.reshape(-1, 1).astype(jnp.float32) * dy_rows.astype(jnp.float32)).astype(
        jnp.bfloat16
    )
    hidden_grad = lax.dot_general(
        scaled, full_down[0], (((1,), (1,)), ((), ())), preferred_element_type=jnp.float32
    )
    down_term = lax.dot_general(
        hidden, scaled, (((0,), (0,)), ((), ())), preferred_element_type=jnp.float32
    )
    gate_grad = (
        hidden_grad * up_pre * sigmoid_gate * (1.0 + gate_pre * (1.0 - sigmoid_gate))
    ).astype(jnp.bfloat16)
    up_grad = (hidden_grad * activated).astype(jnp.bfloat16)
    row_grad = lax.dot_general(
        gate_grad, full_gate, (((1,), (1,)), ((), ())), preferred_element_type=jnp.float32
    )
    row_grad = row_grad + lax.dot_general(
        up_grad, full_up, (((1,), (1,)), ((), ())), preferred_element_type=jnp.float32
    )
    returned = lax.all_to_all(
        row_grad.astype(jnp.bfloat16).reshape(experts, capacity, model_width),
        "expert",
        split_axis=0,
        concat_axis=0,
        tiled=True,
    )
    picked = returned.reshape(experts * capacity, model_width)[slot_index]
    token_grad = jnp.sum(
        picked.astype(jnp.float32).reshape(tok_dev, fan_out, model_width), axis=1
    ).astype(jnp.bfloat16)
    gate_term = lax.dot_general(
        x_rows, gate_grad, (((0,), (0,)), ((), ())), preferred_element_type=jnp.float32
    )
    up_term = lax.dot_general(
        x_rows, up_grad, (((0,), (0,)), ((), ())), preferred_element_type=jnp.float32
    )
    gate_sum, up_sum, down_sum = (
        lax.psum_scatter(
            gate_term[None].astype(jnp.bfloat16), "dp", scatter_dimension=1, tiled=True
        ).astype(jnp.float32),
        lax.psum_scatter(
            up_term[None].astype(jnp.bfloat16), "dp", scatter_dimension=1, tiled=True
        ).astype(jnp.float32),
        lax.psum_scatter(
            down_term[None].astype(jnp.bfloat16), "dp", scatter_dimension=2, tiled=True
        ).astype(jnp.float32),
    )
    return (
        token_grad,
        gate_sum.astype(jnp.bfloat16),
        up_sum.astype(jnp.bfloat16),
        down_sum.astype(jnp.bfloat16),
    )


def solution(mesh):
    in_specs = (
        P(("expert", "dp"), None),
        P(("expert", "dp"), None),
        P(("expert", "dp"), None),
        P(("expert", "dp"), None),
        P("expert", "dp", None),
        P("expert", "dp", None),
        P("expert", None, "dp"),
    )
    out_specs = (
        P(("expert", "dp"), None),
        P("expert", "dp", None),
        P("expert", "dp", None),
        P("expert", None, "dp"),
    )
    small = mesh.shape["expert"] == 8 and mesh.shape["dp"] == 4
    local = one_kernel if small else exchanged
    return jax.shard_map(local, mesh=mesh, in_specs=in_specs, out_specs=out_specs, check_vma=False)
```
